256 devices in a mesh: ctx: 64 (over x, y_hi, z), head: 4 (over y_lo, core).
Axes of the slice: x: 4, y: 4 (y_hi: 2, y_lo: 2; y = y_hi * 2 + y_lo), z: 8, core: 2. Of those that a mesh axis runs over, the one named last changes fastest.
Arguments:
- queries: bfloat16 [4096, 64, 576], P('ctx', 'head'), may hold values from -128 to 128
- latent: bfloat16 [4096, 576], P('ctx'), may hold values from -32 to 32
- documents: int32 [4096], replicated, may hold values from 0 to 5, never falling along the last dimension, each value on 1 to 2048 neighbouring positions
- span_order: int32 [128], replicated, may hold values from 0 to 127, each once
- w_uv: bfloat16 [64, 512, 128], P('head'), may hold values from -0.25 to 0.25
- w_out: bfloat16 [8192, 7168], P('head', 'ctx'), may hold values from -0.0625 to 0.0625
Outputs:
- attn_out: bfloat16 [4096, 7168], P('ctx', 'head')
The draws below stay inside these ranges and needn't reach their ends.
Inputs may be any that keep to these rules, and one draw needn't show every extreme that they name: `documents`: document numbers never fall along the sequence; the longest document holds half of the 4096 positions. `span_order`: each span number appears once.
All inputs are finite; a program needn't handle non-finite values.
Results may differ from the reference program's by a relative error of at most 0.017.
Values may be sent and summed in bfloat16 or wider, within the bound.
No kernel may reach another device: no remote copies, remote signals or barrier semaphores. Data moves between devices by JAX's collectives and lax.ppermute only.
A program may use at most 128 MiB of HBM per device.

```python
import math
import jax
import jax.numpy as jnp
import numpy as np
from jax import lax

D = 7168
KV_RANK = 512
ROPE = 64
VD = 128
TOK_DEV = 64
DOCS = 6
TOKENS = 4096
HEADS = 64
LAT = 576
N_CTX = 64


query_spread = 0.1


def shared_rows(key, scale_low, scale_high, planting):
    keys_all = jax.random.split(key, 3)
    normal_part = jnp.clip(jax.random.normal(keys_all[0], (TOKENS, LAT), jnp.float32), -4.5, 4.5)
    base_rows = normal_part
    row_scale = jnp.exp(jax.random.uniform(keys_all[2], (TOKENS, 1), jnp.float32, math.log(scale_low), math.log(scale_high)))
    row_index = jnp.arange(TOKENS, dtype=jnp.int32)
    planted = (row_index % TOK_DEV >= TOK_DEV - 2).astype(jnp.float32)[:, None] * planting
    value_part = base_rows[:, :KV_RANK] * ((1.0 - planted) * row_scale)
    rope_part = (1.0 - planted) * base_rows[:, KV_RANK:]
    return jnp.concatenate([value_part, rope_part], axis=1)


def draw_latent(key, part):
    rows_made = shared_rows(key, 0.5, 5.0, 0.0)
    return rows_made.astype(jnp.bfloat16)


def draw_queries(key, part):
    planting = 0.0
    key = jax.random.fold_in(key, 11)
    split_keys = jax.random.split(key, 1)
    normal_part = jnp.clip(jax.random.normal(split_keys[0], (TOKENS, HEADS, LAT), jnp.float32), -4.5, 4.5)
    base_query = query_spread * normal_part
    row_index = jnp.arange(TOKENS, dtype=jnp.int32)
    chosen = (row_index % TOK_DEV == TOK_DEV - 1).astype(jnp.float32)[:, None, None] * planting
    return ((1.0 - chosen) * base_query).astype(jnp.bfloat16)


def levels(stream_key, dims, pieces, smallest, largest):
    def one(axis_at, parts):
        heights = jax.random.uniform(jax.random.fold_in(jax.random.fold_in(stream_key, 6), axis_at), (parts,), jnp.float32, smallest / len(pieces), largest / len(pieces))
        return jnp.repeat(jnp.exp(heights), dims[axis_at] // parts).reshape((-1,) + (1,) * (len(dims) - axis_at - 1))

    level = one(*pieces[0])
    for cut in pieces[1:]:
        level = level * one(*cut)
    return level


def split_up(amount, total, bound, skew):
    weights = [(1 << 20) // math.isqrt(rank ** skew) + 1 for rank in range(2, amount + 1)]
    surplus, counts = total - bound - (amount - 1), [1] * (amount - 1)
    while surplus > 0:
        candidates = [i for i in range(amount - 1) if counts[i] < bound]
        mass, remaining = sum([weights[i] for i in candidates]), surplus
        for i in candidates:
            addition = min(bound - counts[i], max(1, remaining * weights[i] // mass), surplus)
            counts[i] = counts[i] + addition
            surplus = surplus - addition
    return np.array([bound] + counts)


def uneven(stream_key, amount, total, reach, lean):
    if amount == 2:
        one = jax.random.randint(stream_key, (), max(1, total - reach), min(reach, total - 1) + 1)
        return jnp.stack([one, total - one])
    tallies = jnp.asarray(split_up(amount, total, reach, lean), jnp.int32)
    twos = (amount - 1) // 2
    giver, receiver = tallies[1:1 + 2 * twos:2], tallies[2:2 + 2 * twos:2]
    margin = jnp.minimum(giver - 1, reach - receiver)
    passed = jax.random.randint(jax.random.fold_in(stream_key, 1), (twos,), 0, 1 << 20) % (margin + 1)
    tallies = tallies.at[1:1 + 2 * twos:2].set(giver - passed).at[2:2 + 2 * twos:2].set(receiver + passed)
    return tallies[jax.random.permutation(jax.random.fold_in(stream_key, 2), amount)]


def gaussian(rng, shape, deviation, limit, cuts=(), kind=jnp.bfloat16):
    result = deviation * jax.random.normal(rng, shape, jnp.float32)
    if cuts:
        result = result * levels(rng, shape, cuts, -0.22, 0.18)
    return jnp.clip(result, -limit, limit).astype(kind)


def setup_inputs(seed: int = 0) -> dict:
    seeds = jax.random.split(jax.random.key(seed), 7)
    return {
        "queries": draw_queries(jax.random.fold_in(seeds[6], 71), 0),
        "latent": draw_latent(jax.random.fold_in(seeds[6], 71), 0),
        "documents": jnp.searchsorted(jnp.cumsum(uneven(seeds[2], DOCS, TOKENS, TOKENS // 2, 0)), jnp.arange(TOKENS), side="right").astype(jnp.int32),
        "span_order": jax.random.permutation(seeds[3], 2 * N_CTX).astype(jnp.int32),
        "w_uv": gaussian(seeds[4], (HEADS, KV_RANK, VD), KV_RANK ** -0.5, 0.25, ((0, 4),)),
        "w_out": gaussian(seeds[5], (HEADS * VD, D), (HEADS * VD) ** -0.5, 0.0625, ((0, 4), (1, 64))),
    }


def stored_layout(documents, span_order, span_rows):
    offsets = jnp.arange(span_rows, dtype=jnp.int32)
    positions = (span_order[:, None] * span_rows + offsets[None, :]).reshape(-1)
    doc_table = documents.reshape(-1, span_rows)
    stored_docs = jnp.take(doc_table, span_order, axis=0).reshape(-1)
    return positions, stored_docs


def reference(queries, latent, documents, span_order, w_uv, w_out):
    span_rows = TOK_DEV // 2
    score_scale = (VD + ROPE) ** -0.5
    positions, stored_docs = stored_layout(documents, span_order, span_rows)
    visible = (stored_docs[:, None] == stored_docs[None, :]) & (positions[None, :] <= positions[:, None])
    values = latent[:, :KV_RANK]

    def one_head(operands):
        query_head, weight_head = operands
        scores = jnp.dot(query_head, latent.T, preferred_element_type=jnp.float32) * score_scale
        scores = jnp.where(visible, scores, -1e30)
        row_max = jnp.max(scores, axis=1, keepdims=True)
        weights = jnp.where(visible, jnp.exp(scores - row_max), 0.0)
        totals = jnp.sum(weights, axis=1, keepdims=True)
        mixed = jnp.dot(weights.astype(jnp.bfloat16), values, preferred_element_type=jnp.float32) / totals
        return jnp.dot(mixed.astype(jnp.bfloat16), weight_head, preferred_element_type=jnp.float32).astype(jnp.bfloat16)

    head_out = lax.map(one_head, (jnp.swapaxes(queries, 0, 1), w_uv))
    flat_heads = jnp.swapaxes(head_out, 0, 1).reshape(TOKENS, HEADS * VD)
    return jnp.dot(flat_heads, w_out, preferred_element_type=jnp.float32).astype(jnp.bfloat16)
```

```python
import functools

import jax
import jax.numpy as jnp
from jax import lax
from jax.experimental import pallas as pl
from jax.experimental.pallas import tpu as pltpu
from jax.sharding import Mesh, PartitionSpec as P

ROPE = 64
VD = 128
DOCS = 6
AXES = ("x", "yh", "z", "yl", "c")
SIZES = (4, 2, 8, 2, 2)
SPAN = 32
GROUP = 8
KEYS = SPAN * GROUP
MAXB = 9
NEG = -1e30


def attention_kernel(
    starts, order, own_slot, q_ref, w_hbm, own_hbm, oth_hbm, out_ref,
    place, k_buf, s_buf, top_buf, sum_buf, acc, mixed, w_buf, k_sem, w_sem,
):
    span_total = order.shape[0]
    heads = q_ref.shape[1]
    rows = SPAN * heads
    value_cols = w_hbm.shape[1]
    scale = (VD + ROPE) ** (-0.5) * 1.4426950408889634
    core = own_slot[1]

    w_copy = pltpu.make_async_copy(w_hbm, w_buf, w_sem)
    w_copy.start()

    def note(s, carry):
        place[order[s]] = s
        return carry

    lax.fori_loop(0, span_total, note, 0)

    def doc_start(pos):
        lo = jnp.zeros_like(pos)
        for d in range(DOCS):
            lo = jnp.maximum(lo, jnp.where(starts[d] <= pos, starts[d], 0))
        return lo

    def plan(t):
        last = order[own_slot[0] * 2 + t]
        lo = jnp.int32(0)
        for d in range(DOCS):
            lo = jnp.maximum(lo, jnp.where(starts[d] <= last * SPAN, starts[d], 0))
        first = lo // SPAN
        return last, first, (last - first + GROUP) // GROUP

    def fetch(t):
        last, first, blocks = plan(t)

        def one(i, carry):
            stored = place[jnp.minimum(first + i, span_total - 1)]
            row = pl.multiple_of(i * SPAN, SPAN)
            dst = k_buf.at[t, pl.ds(row, SPAN)]

            @pl.when(lax.rem(stored, 2) == core)
            def _():
                pltpu.make_async_copy(own_hbm.at[stored // 2], dst, k_sem.at[t, i // GROUP]).start()

            @pl.when(lax.rem(stored, 2) != core)
            def _():
                pltpu.make_async_copy(oth_hbm.at[stored // 2], dst, k_sem.at[t, i // GROUP]).start()

            return carry

        lax.fori_loop(0, blocks * GROUP, one, 0)

    fetch(0)
    fetch(1)

    for t in range(2):
        last, first, blocks = plan(t)
        row_token = lax.broadcasted_iota(jnp.int32, (rows, 1), 0) // heads
        q_pos = last * SPAN + row_token
        q_lo = doc_start(q_pos) - first * SPAN
        q_hi = q_pos - first * SPAN
        q = q_ref[t * SPAN : (t + 1) * SPAN].reshape(rows, q_ref.shape[2])
        top_buf[...] = jnp.full(top_buf.shape, NEG, jnp.float32)
        sum_buf[...] = jnp.zeros(sum_buf.shape, jnp.float32)
        acc[...] = jnp.zeros(acc.shape, jnp.float32)

        def score(b, carry):
            row = pl.multiple_of(b * KEYS, KEYS)
            block = k_buf.at[t, pl.ds(row, KEYS)]
            pltpu.make_async_copy(block, block, k_sem.at[t, b]).wait()
            s = lax.dot_general(
                q, block[...], (((1,), (1,)), ((), ())), preferred_element_type=jnp.float32
            )
            k_pos = b * KEYS + lax.broadcasted_iota(jnp.int32, (1, KEYS), 1)
            s = jnp.where((k_pos >= q_lo) & (k_pos <= q_hi), s, NEG)
            s_buf[b] = s
            top_buf[...] = jnp.maximum(top_buf[...], jnp.maximum(s[:, :128], s[:, 128:]))
            return carry

        lax.fori_loop(0, blocks, score, 0)
        top = jnp.max(top_buf[...], axis=1, keepdims=True)

        def mix(b, carry):
            row = pl.multiple_of(b * KEYS, KEYS)
            w = jnp.exp2((s_buf[b] - top) * scale)
            sum_buf[...] += w[:, :128] + w[:, 128:]
            acc[...] += jnp.dot(
                w.astype(jnp.bfloat16),
                k_buf[t, pl.ds(row, KEYS), :value_cols],
                preferred_element_type=jnp.float32,
            )
            return carry

        lax.fori_loop(0, blocks, mix, 0)
        total = jnp.sum(sum_buf[...], axis=1, keepdims=True)
        scaled = acc[...] / total
        for j in range(value_cols // 128):
            mixed[j, t * rows : (t + 1) * rows, :] = scaled[:, j * 128 : (j + 1) * 128]

    w_copy.wait()
    tokens = 2 * SPAN
    for h in range(heads):
        part = jnp.concatenate(
            [mixed[j, pl.ds(h, tokens, stride=heads), :] for j in range(value_cols // 128)], axis=1
        ).astype(jnp.bfloat16)
        out_ref[:, h * VD : (h + 1) * VD] = jnp.dot(
            part, w_buf[h], preferred_element_type=jnp.float32
        ).astype(jnp.bfloat16)


def attention(starts, order, own_slot, queries, w_uv, own, oth):
    tokens, heads, lat = queries.shape
    value_cols = w_uv.shape[1]
    rows = SPAN * heads
    smem = pl.BlockSpec(memory_space=pltpu.SMEM)
    vmem = pl.BlockSpec(memory_space=pltpu.VMEM)
    hbm = pl.BlockSpec(memory_space=pl.ANY)
    return pl.pallas_call(
        attention_kernel,
        out_shape=jax.ShapeDtypeStruct((tokens, heads * VD), jnp.bfloat16),
        in_specs=[smem, smem, smem, vmem, hbm, hbm, hbm],
        out_specs=vmem,
        scratch_shapes=[
            pltpu.SMEM((order.shape[0],), jnp.int32),
            pltpu.VMEM((2, MAXB * KEYS, lat), jnp.bfloat16),
            pltpu.VMEM((MAXB, rows, KEYS), jnp.float32),
            pltpu.VMEM((rows, 128), jnp.float32),
            pltpu.VMEM((rows, 128), jnp.float32),
            pltpu.VMEM((rows, value_cols), jnp.float32),
            pltpu.VMEM((value_cols // 128, 2 * rows, 128), jnp.float32),
            pltpu.VMEM(w_uv.shape, jnp.bfloat16),
            pltpu.SemaphoreType.DMA((2, MAXB)),
            pltpu.SemaphoreType.DMA(()),
        ],
        compiler_params=pltpu.CompilerParams(vmem_limit_bytes=40 * 2**20),
        cost_estimate=pl.CostEstimate(
            flops=5_000_000_000, bytes_accessed=8_000_000, transcendentals=2_000_000
        ),
    )(starts, order, own_slot, queries, w_uv, own, oth)


def gather_rows(v, axes, count):
    return lax.all_to_all(jnp.broadcast_to(v[None], (count,) + v.shape), axes, 0, 0)


def shards(queries, latent, documents, span_order, w_uv, w_out):
    row_axes = ("x", "yh")
    row_count = 8
    ai = lax.axis_index
    core = ai("c")
    place = ai("x") * 2 + ai("yh")

    w_cols = lax.all_gather(w_out.T, "z", axis=0, tiled=True)

    span = lax.dynamic_slice_in_dim(latent, core * SPAN, SPAN)
    line = gather_rows(span, "z", 8)
    own = gather_rows(line, row_axes, row_count).reshape(64, SPAN, latent.shape[1])
    oth = lax.ppermute(own, "c", [(0, 1), (1, 0)])

    starts = jnp.sum(
        documents[None, :] < jnp.arange(DOCS, dtype=jnp.int32)[:, None], axis=1, dtype=jnp.int32
    )
    own_slot = jnp.stack([place * 8 + ai("z"), core]).astype(jnp.int32)
    head_out = attention(starts, span_order, own_slot, queries, w_uv, own, oth)

    tokens = head_out.shape[0]
    rows = gather_rows(head_out, row_axes, row_count).reshape(row_count * tokens, head_out.shape[1])
    terms = lax.dot_general(
        rows, w_cols, (((1,), (1,)), ((), ())), preferred_element_type=jnp.float32
    ).astype(jnp.bfloat16)
    width = terms.shape[1]
    terms = terms.reshape(2, 4, tokens, width)

    kept = lax.dynamic_index_in_dim(terms, core, 0, keepdims=False)
    sent = lax.dynamic_index_in_dim(terms, 1 - core, 0, keepdims=False)
    got = lax.ppermute(sent, "c", [(0, 1), (1, 0)])
    both = (kept.astype(jnp.float32) + got.astype(jnp.float32)).astype(jnp.bfloat16)

    slot = (place % 2) * 2 + ai("yl")
    left = jnp.zeros((tokens, width), jnp.float32)
    right = left
    for k in range(4):
        pairs = []
        for r in range(8):
            for yl in range(2):
                for c in range(2):
                    i = ((r % 2) * 2 + yl + k) % 4
                    pairs.append((r * 4 + yl * 2 + c, (c * 4 + i) * 4 + r // 2))
        block = lax.dynamic_index_in_dim(both, (slot + k) % 4, 0, keepdims=False)
        got = lax.ppermute(block, ("x", "yh", "yl", "c"), pairs).astype(jnp.float32)
        first_half = (place - k) % 4 < 2
        left = left + jnp.where(first_half, got, 0.0)
        right = right + jnp.where(first_half, 0.0, got)
    return jnp.concatenate([left, right], axis=1).astype(jnp.bfloat16)


def solution(mesh):
    fine = Mesh(mesh.devices.reshape(SIZES), AXES)
    ctx, head = ("x", "yh", "z"), ("yl", "c")
    return jax.shard_map(
        shards,
        mesh=fine,
        in_specs=(
            P(ctx, head, None),
            P(ctx, None),
            P(),
            P(),
            P(head, None, None),
            P(head, ctx),
        ),
        out_specs=P(ctx, head),
        check_vma=False,
    )
```

```python
import functools

import jax
import jax.numpy as jnp
from jax import lax
from jax.experimental import pallas as pl
from jax.experimental.pallas import tpu as pltpu
from jax.sharding import Mesh, PartitionSpec as P

ROPE = 64
VD = 128
DOCS = 6
AXES = ("x", "yh", "z", "yl", "c")
SIZES = (4, 2, 8, 2, 2)
SPAN = 32
GROUP = 16
KEYS = SPAN * GROUP
MAXB = 5
NEG = -1e30
COPIES = 8


def attention_kernel(
    starts, place, slot, q_ref, w_hbm, own_ref, oth_ref, out_ref,
    k_buf, s_buf, top_buf, sum_buf, acc, mixed, w_buf, w_sem,
):
    span_total = place.shape[0]
    heads = q_ref.shape[1]
    rows = SPAN * heads
    value_cols = w_hbm.shape[1]
    scale = (VD + ROPE) ** (-0.5) * 1.4426950408889634
    core = slot[2]

    w_copy = pltpu.make_async_copy(w_hbm, w_buf, w_sem)
    w_copy.start()

    def doc_start(pos):
        lo = jnp.zeros_like(pos)
        for d in range(DOCS):
            lo = jnp.maximum(lo, jnp.where(starts[d] <= pos, starts[d], 0))
        return lo

    for t in range(2):
        last = slot[t]
        lo = jnp.int32(0)
        for d in range(DOCS):
            lo = jnp.maximum(lo, jnp.where(starts[d] <= last * SPAN, starts[d], 0))
        first = lo // SPAN
        blocks = (last - first + GROUP) // GROUP
        row_token = lax.broadcasted_iota(jnp.int32, (rows, 1), 0) // heads
        q_pos = last * SPAN + row_token
        q_lo = doc_start(q_pos) - first * SPAN
        q_hi = q_pos - first * SPAN
        q = q_ref[t * SPAN : (t + 1) * SPAN].reshape(rows, q_ref.shape[2])
        top_buf[...] = jnp.full(top_buf.shape, NEG, jnp.float32)
        sum_buf[...] = jnp.zeros(sum_buf.shape, jnp.float32)
        acc[...] = jnp.zeros(acc.shape, jnp.float32)

        def score(b, carry):
            for g in range(GROUP):
                stored = place[jnp.minimum(first + b * GROUP + g, span_total - 1)]
                mine = lax.rem(stored, 2) == core
                k_buf[b, g * SPAN : (g + 1) * SPAN] = jnp.where(
                    mine, own_ref[stored // 2], oth_ref[stored // 2]
                )
            s = lax.dot_general(
                q, k_buf[b], (((1,), (1,)), ((), ())), preferred_element_type=jnp.float32
            )
            k_pos = b * KEYS + lax.broadcasted_iota(jnp.int32, (1, KEYS), 1)
            s = jnp.where((k_pos >= q_lo) & (k_pos <= q_hi), s, NEG)
            s_buf[b] = s
            top = top_buf[...]
            for j in range(KEYS // 128):
                top = jnp.maximum(top, s[:, j * 128 : (j + 1) * 128])
            top_buf[...] = top
            return carry

        lax.fori_loop(0, blocks, score, 0)
        top = jnp.max(top_buf[...], axis=1, keepdims=True)

        def mix(b, carry):
            w = jnp.exp2((s_buf[b] - top) * scale)
            part = sum_buf[...]
            for j in range(KEYS // 128):
                part = part + w[:, j * 128 : (j + 1) * 128]
            sum_buf[...] = part
            acc[...] += jnp.dot(
                w.astype(jnp.bfloat16), k_buf[b, :, :value_cols], preferred_element_type=jnp.float32
            )
            return carry

        lax.fori_loop(0, blocks, mix, 0)
        total = jnp.sum(sum_buf[...], axis=1, keepdims=True)
        scaled = acc[...] / total
        for j in range(value_cols // 128):
            mixed[j, t * rows : (t + 1) * rows, :] = scaled[:, j * 128 : (j + 1) * 128]

    w_copy.wait()
    tokens = 2 * SPAN
    for h in range(heads):
        part = jnp.concatenate(
            [mixed[j, pl.ds(h, tokens, stride=heads), :] for j in range(value_cols // 128)], axis=1
        ).astype(jnp.bfloat16)
        piece = jnp.dot(part, w_buf[h], preferred_element_type=jnp.float32).astype(jnp.bfloat16)
        for r in range(out_ref.shape[0]):
            out_ref[r, :, h * VD : (h + 1) * VD] = piece


def attention(starts, place, slot, queries, w_uv, own, oth):
    tokens, heads, lat = queries.shape
    value_cols = w_uv.shape[1]
    rows = SPAN * heads
    smem = pl.BlockSpec(memory_space=pltpu.SMEM)
    vmem = pl.BlockSpec(memory_space=pltpu.VMEM)
    hbm = pl.BlockSpec(memory_space=pl.ANY)
    return pl.pallas_call(
        attention_kernel,
        out_shape=jax.ShapeDtypeStruct((COPIES, tokens, heads * VD), jnp.bfloat16),
        in_specs=[smem, smem, smem, vmem, hbm, vmem, vmem],
        out_specs=vmem,
        scratch_shapes=[
            pltpu.VMEM((MAXB, KEYS, lat), jnp.bfloat16),
            pltpu.VMEM((MAXB, rows, KEYS), jnp.float32),
            pltpu.VMEM((rows, 128), jnp.float32),
            pltpu.VMEM((rows, 128), jnp.float32),
            pltpu.VMEM((rows, value_cols), jnp.float32),
            pltpu.VMEM((value_cols // 128, 2 * rows, 128), jnp.float32),
            pltpu.VMEM(w_uv.shape, jnp.bfloat16),
            pltpu.SemaphoreType.DMA(()),
        ],
        compiler_params=pltpu.CompilerParams(vmem_limit_bytes=40 * 2**20),
        cost_estimate=pl.CostEstimate(
            flops=5_000_000_000, bytes_accessed=8_000_000, transcendentals=2_000_000
        ),
    )(starts, place, slot, queries, w_uv, own, oth)


def gather_rows(v, axes, count):
    return lax.all_to_all(jnp.broadcast_to(v[None], (count,) + v.shape), axes, 0, 0)


def shards(queries, latent, documents, span_order, w_uv, w_out):
    row_axes = ("x", "yh")
    ai = lax.axis_index
    core, zi = ai("c"), ai("z")
    place = ai("x") * 2 + ai("yh")
    tie = lax.optimization_barrier

    def shift(v, k):
        return lax.ppermute(v, "z", [(i, (i + k) % 8) for i in range(8)])

    w_own = w_out.T
    half = 64
    span = lax.dynamic_slice_in_dim(latent, core * SPAN, SPAN)
    line = gather_rows(span, "z", 8)
    line, w_own = tie((line, w_own))

    up1, down1 = shift(w_own, 1), shift(w_own, -1)
    up2, down2 = shift(up1, 1), shift(down1, -1)
    own = gather_rows(line, row_axes, COPIES).reshape(64, SPAN, latent.shape[1])
    own, up2, down2 = tie((own, up2, down2))

    up3, down3 = shift(up2, 1), shift(down2, -1)
    oth = lax.ppermute(own, "c", [(0, 1), (1, 0)])
    starts = jnp.sum(
        documents[None, :] < jnp.arange(DOCS, dtype=jnp.int32)[:, None], axis=1, dtype=jnp.int32
    )
    spans = jnp.arange(span_order.shape[0], dtype=jnp.int32)
    stored = jnp.sum(jnp.where(span_order[None, :] == spans[:, None], spans[None, :], 0), axis=1)
    slot = jnp.concatenate(
        [lax.dynamic_slice_in_dim(span_order, 2 * (place * 8 + zi), 2), core[None].astype(jnp.int32)]
    )
    head_out = attention(starts, stored, slot, queries, w_uv, own, oth)
    head_out, up3, down3 = tie((head_out, up3, down3))

    far = jnp.concatenate([shift(up3[:half], 1), shift(down3[half:], -1)], axis=0)
    tokens = head_out.shape[1]
    rows = lax.all_to_all(head_out, row_axes, 0, 0).reshape(COPIES * tokens, head_out.shape[2])
    w_all = jnp.zeros((8,) + w_own.shape, w_own.dtype)
    for k, v in enumerate((w_own, up1, up2, up3, far, down3, down2, down1)):
        w_all = lax.dynamic_update_index_in_dim(w_all, v, (zi - k) % 8, 0)
    w_cols = w_all.reshape(-1, w_own.shape[1])
    terms = lax.dot_general(
        rows, w_cols, (((1,), (1,)), ((), ())), preferred_element_type=jnp.float32
    ).astype(jnp.bfloat16)
    width = terms.shape[1]
    terms = terms.reshape(2, 4, tokens, width)

    kept = lax.dynamic_index_in_dim(terms, core, 0, keepdims=False)
    sent = lax.dynamic_index_in_dim(terms, 1 - core, 0, keepdims=False)
    got = lax.ppermute(sent, "c", [(0, 1), (1, 0)])
    both = (kept.astype(jnp.float32) + got.astype(jnp.float32)).astype(jnp.bfloat16)

    slot = (place % 2) * 2 + ai("yl")
    left = jnp.zeros((tokens, width), jnp.float32)
    right = left
    for k in range(4):
        pairs = []
        for r in range(8):
            for yl in range(2):
                for c in range(2):
                    i = ((r % 2) * 2 + yl + k) % 4
                    pairs.append((r * 4 + yl * 2 + c, (c * 4 + i) * 4 + r // 2))
        block = lax.dynamic_index_in_dim(both, (slot + k) % 4, 0, keepdims=False)
        got = lax.ppermute(block, ("x", "yh", "yl", "c"), pairs).astype(jnp.float32)
        first_half = (place - k) % 4 < 2
        left = left + jnp.where(first_half, got, 0.0)
        right = right + jnp.where(first_half, 0.0, got)
    return jnp.concatenate([left, right], axis=1).astype(jnp.bfloat16)


def solution(mesh):
    fine = Mesh(mesh.devices.reshape(SIZES), AXES)
    ctx, head = ("x", "yh", "z"), ("yl", "c")
    return jax.shard_map(
        shards,
        mesh=fine,
        in_specs=(
            P(ctx, head, None),
            P(ctx, None),
            P(),
            P(),
            P(head, None, None),
            P(head, ctx),
        ),
        out_specs=P(ctx, head),
        check_vma=False,
    )
```

```python
import functools

import jax
import jax.numpy as jnp
from jax import lax
from jax.experimental import pallas as pl
from jax.experimental.pallas import tpu as pltpu
from jax.sharding import Mesh, PartitionSpec as P

ROPE = 64
VD = 128
DOCS = 6
AXES = ("x", "yh", "z", "yl", "c")
SIZES = (4, 2, 8, 2, 2)
SPAN = 32
HALF = SPAN // 2
GROUP = 16
KEYS = SPAN * GROUP
MAXB = 5
NEG = -1e30
COPIES = 8


def attention_kernel(
    starts, place, slot, q_hbm, w_hbm, own_ref, oth_ref, out_ref,
    k_buf, s_buf, top_buf, sum_buf, acc, mixed, q_ref, w_buf, head_out, q_sem, w_sem, out_sem,
):
    span_total = place.shape[0]
    heads = q_hbm.shape[1]
    q_copy = pltpu.make_async_copy(q_hbm, q_ref, q_sem)
    q_copy.start()
    rows = SPAN * heads
    value_cols = w_hbm.shape[1]
    scale = (VD + ROPE) ** (-0.5) * 1.4426950408889634
    core = slot[2]
    line_rows = 8 * HALF
    low_lanes = lax.broadcasted_iota(jnp.int32, (HALF, 2 * ROPE), 1) < ROPE

    w_copy = pltpu.make_async_copy(w_hbm, w_buf, w_sem)
    w_copy.start()

    def doc_start(pos):
        lo = jnp.zeros_like(pos)
        for d in range(DOCS):
            lo = jnp.maximum(lo, jnp.where(starts[d] <= pos, starts[d], 0))
        return lo

    lane = lax.broadcasted_iota(jnp.int32, (1, KEYS), 1)
    key_half = jnp.where(lane < KEYS // 2, core, 1 - core)
    key_place = ((lane & (KEYS // 2 - 1)) >> 4) * SPAN + key_half * HALF + (lane & (HALF - 1))

    for t in range(2):
        last = slot[t]
        lo = jnp.int32(0)
        for d in range(DOCS):
            lo = jnp.maximum(lo, jnp.where(starts[d] <= last * SPAN, starts[d], 0))
        first = lo // SPAN
        blocks = (last - first + GROUP) // GROUP
        row_token = lax.broadcasted_iota(jnp.int32, (rows, 1), 0) // heads
        q_pos = last * SPAN + row_token
        q_lo = doc_start(q_pos) - first * SPAN
        q_hi = q_pos - first * SPAN
        if t == 0:
            q_copy.wait()
        q = q_ref[t * SPAN : (t + 1) * SPAN].reshape(rows, q_ref.shape[2])
        q = jnp.concatenate([q, q[:, value_cols:]], axis=1)
        top_buf[...] = jnp.full(top_buf.shape, NEG, jnp.float32)
        sum_buf[...] = jnp.zeros(sum_buf.shape, jnp.float32)
        acc[...] = jnp.zeros(acc.shape, jnp.float32)

        def score(b, carry):
            for g in range(GROUP):
                code = place[jnp.minimum(first + b * GROUP + g, span_total - 1)]
                block = lax.shift_right_logical(code, 3)
                z = code & 7
                for i, ref in enumerate((own_ref, oth_ref)):
                    row = i * KEYS // 2 + g * HALF
                    for j in range(value_cols // 128):
                        src = pl.multiple_of(j * line_rows + z * HALF, HALF)
                        k_buf[b, row : row + HALF, j * 128 : (j + 1) * 128] = ref[
                            block, pl.ds(src, HALF)
                        ]
                    src = pl.multiple_of(value_cols // 128 * line_rows + (z & 3) * HALF, HALF)
                    rope = ref[block, pl.ds(src, HALF)]
                    k_buf[b, row : row + HALF, value_cols:] = jnp.where(
                        low_lanes == (z < 4), rope, jnp.zeros_like(rope)
                    )
            s = lax.dot_general(
                q, k_buf[b], (((1,), (1,)), ((), ())), preferred_element_type=jnp.float32
            )
            k_pos = b * KEYS + key_place
            s = jnp.where((k_pos >= q_lo) & (k_pos <= q_hi), s, NEG)
            s_buf[b] = s
            top = top_buf[...]
            for j in range(KEYS // 128):
                top = jnp.maximum(top, s[:, j * 128 : (j + 1) * 128])
            top_buf[...] = top
            return carry

        lax.fori_loop(0, blocks, score, 0)
        top = jnp.max(top_buf[...], axis=1, keepdims=True)

        def mix(b, carry):
            w = jnp.exp2((s_buf[b] - top) * scale)
            part = sum_buf[...]
            for j in range(KEYS // 128):
                part = part + w[:, j * 128 : (j + 1) * 128]
            sum_buf[...] = part
            acc[...] += jnp.dot(
                w.astype(jnp.bfloat16), k_buf[b, :, :value_cols], preferred_element_type=jnp.float32
            )
            return carry

        lax.fori_loop(0, blocks, mix, 0)
        total = jnp.sum(sum_buf[...], axis=1, keepdims=True)
        scaled = acc[...] * (1.0 / total)
        for j in range(value_cols // 128):
            mixed[j, t * rows : (t + 1) * rows, :] = scaled[:, j * 128 : (j + 1) * 128]

    w_copy.wait()
    tokens = 2 * SPAN
    for h in range(0, heads, 2):
        pair = jnp.concatenate(
            [
                jnp.concatenate(
                    [mixed[j, pl.ds(h + i, tokens, stride=heads), :] for j in range(value_cols // 128)],
                    axis=1,
                )
                for i in range(2)
            ],
            axis=0,
        ).astype(jnp.bfloat16)
        both = jnp.dot(
            pair,
            jnp.concatenate([w_buf[h], w_buf[h + 1]], axis=1),
            preferred_element_type=jnp.float32,
        ).astype(jnp.bfloat16)
        head_out[:, h * VD : (h + 1) * VD] = both[:tokens, :VD]
        head_out[:, (h + 1) * VD : (h + 2) * VD] = both[tokens:, VD:]
    copies = [
        pltpu.make_async_copy(head_out, out_ref.at[r], out_sem.at[r])
        for r in range(out_ref.shape[0])
    ]
    for copy in copies:
        copy.start()
    for copy in copies:
        copy.wait()


def attention(starts, place, slot, queries, w_uv, own, oth):
    tokens, heads, lat = queries.shape
    value_cols = w_uv.shape[1]
    rows = SPAN * heads
    smem = pl.BlockSpec(memory_space=pltpu.SMEM)
    vmem = pl.BlockSpec(memory_space=pltpu.VMEM)
    hbm = pl.BlockSpec(memory_space=pl.ANY)
    return pl.pallas_call(
        attention_kernel,
        out_shape=jax.ShapeDtypeStruct((COPIES, tokens, heads * VD), jnp.bfloat16),
        in_specs=[smem, smem, smem, hbm, hbm, vmem, vmem],
        out_specs=hbm,
        scratch_shapes=[
            pltpu.VMEM((MAXB, KEYS, lat + ROPE), jnp.bfloat16),
            pltpu.VMEM((MAXB, rows, KEYS), jnp.float32),
            pltpu.VMEM((rows, 128), jnp.float32),
            pltpu.VMEM((rows, 128), jnp.float32),
            pltpu.VMEM((rows, value_cols), jnp.float32),
            pltpu.VMEM((value_cols // 128, 2 * rows, 128), jnp.float32),
            pltpu.VMEM(queries.shape, jnp.bfloat16),
            pltpu.VMEM(w_uv.shape, jnp.bfloat16),
            pltpu.VMEM((tokens, heads * VD), jnp.bfloat16),
            pltpu.SemaphoreType.DMA(()),
            pltpu.SemaphoreType.DMA(()),
            pltpu.SemaphoreType.DMA((COPIES,)),
        ],
        compiler_params=pltpu.CompilerParams(vmem_limit_bytes=50 * 2**20),
        cost_estimate=pl.CostEstimate(
            flops=5_000_000_000, bytes_accessed=8_000_000, transcendentals=2_000_000
        ),
    )(starts, place, slot, queries, w_uv, own, oth)


def pack_kernel(line_ref, out_ref, buf, sem):
    blocks, rows, width = line_ref.shape
    count = blocks * rows
    value_cols = width - ROPE
    for j in range(value_cols // 128):
        buf[j * count : (j + 1) * count] = line_ref[:, :, j * 128 : (j + 1) * 128].reshape(count, 128)
    rope = line_ref[:, :, value_cols:].reshape(count, ROPE)
    first = value_cols // 128 * count
    buf[first : first + count // 2] = jnp.concatenate(
        [rope[: count // 2], rope[count // 2 :]], axis=1
    )
    copies = [
        pltpu.make_async_copy(buf, out_ref.at[r], sem.at[r]) for r in range(out_ref.shape[0])
    ]
    for copy in copies:
        copy.start()
    for copy in copies:
        copy.wait()


def pack(line, count):
    rows = line.shape[0] * line.shape[1] * line.shape[2] // 128
    return pl.pallas_call(
        pack_kernel,
        out_shape=jax.ShapeDtypeStruct((count, rows, 128), jnp.bfloat16),
        in_specs=[pl.BlockSpec(memory_space=pltpu.VMEM)],
        out_specs=pl.BlockSpec(memory_space=pl.ANY),
        scratch_shapes=[
            pltpu.VMEM((rows, 128), jnp.bfloat16),
            pltpu.SemaphoreType.DMA((count,)),
        ],
        compiler_params=pltpu.CompilerParams(vmem_limit_bytes=58 * 2**20),
        cost_estimate=pl.CostEstimate(flops=0, bytes_accessed=3_000_000, transcendentals=0),
    )(line)


def gather_rows(v, axes, count):
    return lax.all_to_all(jnp.broadcast_to(v[None], (count,) + v.shape), axes, 0, 0)


def shards(queries, latent, documents, span_order, w_uv, w_out):
    row_axes = ("x", "yh")
    ai = lax.axis_index
    core, zi = ai("c"), ai("z")
    place = ai("x") * 2 + ai("yh")
    tie = lax.optimization_barrier

    def shift(v, k):
        return lax.ppermute(v, "z", [(i, (i + k) % 8) for i in range(8)])

    w_own = w_out.T
    half = 64
    quarter = ai("yl") * 2 + core
    line = gather_rows(lax.dynamic_slice_in_dim(latent, quarter * HALF, HALF), "z", 8)
    line, w_own = tie((line, w_own))

    up1, down1 = shift(w_own, 1), shift(w_own, -1)
    up2, down2 = shift(up1, 1), shift(down1, -1)
    own = lax.all_to_all(pack(line, 16), ("x", "yh", "yl"), 0, 0)
    up3, down3 = shift(up2, 1), shift(down2, -1)
    w_all = jnp.zeros((8,) + w_own.shape, w_own.dtype)
    for k, v in ((0, w_own), (1, up1), (7, down1)):
        w_all = lax.dynamic_update_index_in_dim(w_all, v, (zi - k) % 8, 0)
    own, up2, down2, w_all = tie((own, up2, down2, w_all))

    oth = lax.ppermute(own, "c", [(0, 1), (1, 0)])
    starts = jnp.sum(
        documents[None, :] < jnp.arange(DOCS, dtype=jnp.int32)[:, None], axis=1, dtype=jnp.int32
    )
    spans = jnp.arange(span_order.shape[0], dtype=jnp.int32)
    where = (spans // 16 * 2 + spans % 2) * 8 + spans // 2 % 8
    stored = jnp.sum(jnp.where(span_order[None, :] == spans[:, None], where[None, :], 0), axis=1)
    slot = jnp.concatenate(
        [lax.dynamic_slice_in_dim(span_order, 2 * (place * 8 + zi), 2), core[None].astype(jnp.int32)]
    )
    head_out = attention(starts, stored, slot, queries, w_uv, own, oth)
    head_out, up3, down3 = tie((head_out, up3, down3))

    far = jnp.concatenate([shift(up3[:half], 1), shift(down3[half:], -1)], axis=0)
    tokens = head_out.shape[1]
    rows = lax.all_to_all(head_out, row_axes, 0, 0).reshape(COPIES * tokens, head_out.shape[2])
    for k, v in ((2, up2), (6, down2), (3, up3), (5, down3), (4, far)):
        w_all = lax.dynamic_update_index_in_dim(w_all, v, (zi - k) % 8, 0)
    w_cols = w_all.reshape(-1, w_own.shape[1])
    terms = lax.dot_general(
        rows, w_cols, (((1,), (1,)), ((), ())), preferred_element_type=jnp.float32
    ).astype(jnp.bfloat16)
    width = terms.shape[1]
    terms = terms.reshape(2, 4, tokens, width)

    kept = lax.dynamic_index_in_dim(terms, core, 0, keepdims=False)
    sent = lax.dynamic_index_in_dim(terms, 1 - core, 0, keepdims=False)
    got = lax.ppermute(sent, "c", [(0, 1), (1, 0)])
    both = (kept.astype(jnp.float32) + got.astype(jnp.float32)).astype(jnp.bfloat16)

    slot = (place % 2) * 2 + ai("yl")
    left = jnp.zeros((tokens, width), jnp.float32)
    right = left
    for k in range(4):
        pairs = []
        for r in range(8):
            for yl in range(2):
                for c in range(2):
                    i = ((r % 2) * 2 + yl + k) % 4
                    pairs.append((r * 4 + yl * 2 + c, (c * 4 + i) * 4 + r // 2))
        block = lax.dynamic_index_in_dim(both, (slot + k) % 4, 0, keepdims=False)
        got = lax.ppermute(block, ("x", "yh", "yl", "c"), pairs).astype(jnp.float32)
        first_half = (place - k) % 4 < 2
        left = left + jnp.where(first_half, got, 0.0)
        right = right + jnp.where(first_half, 0.0, got)
    return jnp.concatenate([left, right], axis=1).astype(jnp.bfloat16)


def solution(mesh):
    fine = Mesh(mesh.devices.reshape(SIZES), AXES)
    ctx, head = ("x", "yh", "z"), ("yl", "c")
    return jax.shard_map(
        shards,
        mesh=fine,
        in_specs=(
            P(ctx, head, None),
            P(ctx, None),
            P(),
            P(),
            P(head, None, None),
            P(head, ctx),
        ),
        out_specs=P(ctx, head),
        check_vma=False,
    )
```

```python
import functools

import jax
import jax.numpy as jnp
from jax import lax
from jax.experimental import pallas as pl
from jax.experimental.pallas import tpu as pltpu
from jax.sharding import Mesh, PartitionSpec as P

ROPE = 64
VD = 128
DOCS = 6
AXES = ("x", "yh", "z", "yl", "c")
SIZES = (4, 2, 8, 2, 2)
SPAN = 32
HALF = SPAN // 2
GROUP = 16
KEYS = SPAN * GROUP
MAXB = 5
NEG = -1e30
COPIES = 8


def attention_kernel(
    starts, place, slot, q_hbm, w_hbm, own_ref, oth_ref, out_ref,
    k_buf, s_buf, top_buf, sum_buf, acc, mixed, q_ref, w_buf, head_out, q_sem, w_sem, out_sem,
):
    span_total = place.shape[0]
    heads = q_hbm.shape[1]
    q_copy = pltpu.make_async_copy(q_hbm, q_ref, q_sem)
    q_copy.start()
    rows = SPAN * heads
    value_cols = w_hbm.shape[1]
    scale = (VD + ROPE) ** (-0.5) * 1.4426950408889634
    core = slot[2]
    line_rows = 8 * HALF
    low_lanes = lax.broadcasted_iota(jnp.int32, (HALF, 2 * ROPE), 1) < ROPE

    w_copy = pltpu.make_async_copy(w_hbm, w_buf, w_sem)
    w_copy.start()

    def doc_start(pos):
        lo = jnp.zeros_like(pos)
        for d in range(DOCS):
            lo = jnp.maximum(lo, jnp.where(starts[d] <= pos, starts[d], 0))
        return lo

    lane = lax.broadcasted_iota(jnp.int32, (1, KEYS), 1)
    key_half = jnp.where(lane < KEYS // 2, core, 1 - core)
    key_place = ((lane & (KEYS // 2 - 1)) >> 4) * SPAN + key_half * HALF + (lane & (HALF - 1))

    for t in range(2):
        last = slot[t]
        lo = jnp.int32(0)
        for d in range(DOCS):
            lo = jnp.maximum(lo, jnp.where(starts[d] <= last * SPAN, starts[d], 0))
        first = lo // SPAN
        blocks = (last - first + GROUP) // GROUP
        row_token = lax.broadcasted_iota(jnp.int32, (rows, 1), 0) // heads
        q_pos = last * SPAN + row_token
        q_lo = doc_start(q_pos) - first * SPAN
        q_hi = q_pos - first * SPAN
        if t == 0:
            q_copy.wait()
        q = q_ref[t * SPAN : (t + 1) * SPAN].reshape(rows, q_ref.shape[2])
        q = jnp.concatenate([q, q[:, value_cols:]], axis=1)
        top_buf[...] = jnp.full(top_buf.shape, NEG, jnp.float32)
        sum_buf[...] = jnp.zeros(sum_buf.shape, jnp.float32)
        acc[...] = jnp.zeros(acc.shape, jnp.float32)

        def score(b, carry):
            for g in range(GROUP):
                code = place[jnp.minimum(first + b * GROUP + g, span_total - 1)]
                block = lax.shift_right_logical(code, 3)
                z = code & 7
                for i, ref in enumerate((own_ref, oth_ref)):
                    row = i * KEYS // 2 + g * HALF
                    for j in range(value_cols // 128):
                        src = pl.multiple_of(j * line_rows + z * HALF, HALF)
                        k_buf[b, row : row + HALF, j * 128 : (j + 1) * 128] = ref[
                            block, pl.ds(src, HALF)
                        ]
                    src = pl.multiple_of(value_cols // 128 * line_rows + (z & 3) * HALF, HALF)
                    rope = ref[block, pl.ds(src, HALF)]
                    k_buf[b, row : row + HALF, value_cols:] = jnp.where(
                        low_lanes == (z < 4), rope, jnp.zeros_like(rope)
                    )
            s = lax.dot_general(
                q, k_buf[b], (((1,), (1,)), ((), ())), preferred_element_type=jnp.float32
            )
            k_pos = b * KEYS + key_place
            s = jnp.where((k_pos >= q_lo) & (k_pos <= q_hi), s, NEG)
            s_buf[b] = s
            top = top_buf[...]
            for j in range(KEYS // 128):
                top = jnp.maximum(top, s[:, j * 128 : (j + 1) * 128])
            top_buf[...] = top
            return carry

        lax.fori_loop(0, blocks, score, 0)
        top = jnp.max(top_buf[...], axis=1, keepdims=True)

        def mix(b, carry):
            w = jnp.exp2((s_buf[b] - top) * scale)
            part = sum_buf[...]
            for j in range(KEYS // 128):
                part = part + w[:, j * 128 : (j + 1) * 128]
            sum_buf[...] = part
            acc[...] += jnp.dot(
                w.astype(jnp.bfloat16), k_buf[b, :, :value_cols], preferred_element_type=jnp.float32
            )
            return carry

        lax.fori_loop(0, blocks, mix, 0)
        total = jnp.sum(sum_buf[...], axis=1, keepdims=True)
        scaled = acc[...] * (1.0 / total)
        for j in range(value_cols // 128):
            mixed[j, t * rows : (t + 1) * rows, :] = scaled[:, j * 128 : (j + 1) * 128]

    w_copy.wait()
    tokens = 2 * SPAN
    for h in range(0, heads, 2):
        pair = jnp.concatenate(
            [
                jnp.concatenate(
                    [mixed[j, pl.ds(h + i, tokens, stride=heads), :] for j in range(value_cols // 128)],
                    axis=1,
                )
                for i in range(2)
            ],
            axis=0,
        ).astype(jnp.bfloat16)
        both = jnp.dot(
            pair,
            jnp.concatenate([w_buf[h], w_buf[h + 1]], axis=1),
            preferred_element_type=jnp.float32,
        ).astype(jnp.bfloat16)
        head_out[:, h * VD : (h + 1) * VD] = both[:tokens, :VD]
        head_out[:, (h + 1) * VD : (h + 2) * VD] = both[tokens:, VD:]
    copies = [
        pltpu.make_async_copy(head_out, out_ref.at[r], out_sem.at[r])
        for r in range(out_ref.shape[0])
    ]
    for copy in copies:
        copy.start()
    for copy in copies:
        copy.wait()


def in_hbm(v):
    return pltpu.with_memory_space_constraint(v, pltpu.HBM)


def attention(starts, place, slot, queries, w_uv, own, oth):
    tokens, heads, lat = queries.shape
    value_cols = w_uv.shape[1]
    rows = SPAN * heads
    smem = pl.BlockSpec(memory_space=pltpu.SMEM)
    vmem = pl.BlockSpec(memory_space=pltpu.VMEM)
    hbm = pl.BlockSpec(memory_space=pl.ANY)
    return pl.pallas_call(
        attention_kernel,
        out_shape=pltpu.HBM((COPIES, tokens, heads * VD), jnp.bfloat16),
        in_specs=[smem, smem, smem, hbm, hbm, vmem, vmem],
        out_specs=hbm,
        scratch_shapes=[
            pltpu.VMEM((MAXB, KEYS, lat + ROPE), jnp.bfloat16),
            pltpu.VMEM((MAXB, rows, KEYS), jnp.float32),
            pltpu.VMEM((rows, 128), jnp.float32),
            pltpu.VMEM((rows, 128), jnp.float32),
            pltpu.VMEM((rows, value_cols), jnp.float32),
            pltpu.VMEM((value_cols // 128, 2 * rows, 128), jnp.float32),
            pltpu.VMEM(queries.shape, jnp.bfloat16),
            pltpu.VMEM(w_uv.shape, jnp.bfloat16),
            pltpu.VMEM((tokens, heads * VD), jnp.bfloat16),
            pltpu.SemaphoreType.DMA(()),
            pltpu.SemaphoreType.DMA(()),
            pltpu.SemaphoreType.DMA((COPIES,)),
        ],
        compiler_params=pltpu.CompilerParams(vmem_limit_bytes=36 * 2**20),
        cost_estimate=pl.CostEstimate(
            flops=5_000_000_000, bytes_accessed=8_000_000, transcendentals=2_000_000
        ),
    )(starts, place, slot, in_hbm(queries), in_hbm(w_uv), own, oth)


def pack_kernel(line_ref, out_ref, buf, sem):
    blocks, rows, width = line_ref.shape
    count = blocks * rows
    value_cols = width - ROPE
    for j in range(value_cols // 128):
        buf[j * count : (j + 1) * count] = line_ref[:, :, j * 128 : (j + 1) * 128].reshape(count, 128)
    rope = line_ref[:, :, value_cols:].reshape(count, ROPE)
    first = value_cols // 128 * count
    buf[first : first + count // 2] = jnp.concatenate(
        [rope[: count // 2], rope[count // 2 :]], axis=1
    )
    copies = [
        pltpu.make_async_copy(buf, out_ref.at[r], sem.at[r]) for r in range(out_ref.shape[0])
    ]
    for copy in copies:
        copy.start()
    for copy in copies:
        copy.wait()


def pack(line, count):
    rows = line.shape[0] * line.shape[1] * line.shape[2] // 128
    return pl.pallas_call(
        pack_kernel,
        out_shape=pltpu.HBM((count, rows, 128), jnp.bfloat16),
        in_specs=[pl.BlockSpec(memory_space=pltpu.VMEM)],
        out_specs=pl.BlockSpec(memory_space=pl.ANY),
        scratch_shapes=[
            pltpu.VMEM((rows, 128), jnp.bfloat16),
            pltpu.SemaphoreType.DMA((count,)),
        ],
        compiler_params=pltpu.CompilerParams(vmem_limit_bytes=16 * 2**20),
        cost_estimate=pl.CostEstimate(flops=0, bytes_accessed=3_000_000, transcendentals=0),
    )(line)


def gather_rows(v, axes, count):
    return lax.all_to_all(jnp.broadcast_to(v[None], (count,) + v.shape), axes, 0, 0)


def shards(queries, latent, documents, span_order, w_uv, w_out):
    row_axes = ("x", "yh")
    ai = lax.axis_index
    core, zi = ai("c"), ai("z")
    place = ai("x") * 2 + ai("yh")
    tie = lax.optimization_barrier

    def shift(v, k):
        return lax.ppermute(v, "z", [(i, (i + k) % 8) for i in range(8)])

    w_own = w_out.T
    half = 64
    quarter = ai("yl") * 2 + core
    line = gather_rows(lax.dynamic_slice_in_dim(latent, quarter * HALF, HALF), "z", 8)
    line, w_own = tie((line, w_own))

    up1, down1 = shift(w_own, 1), shift(w_own, -1)
    up2, down2 = shift(up1, 1), shift(down1, -1)
    own = lax.all_to_all(pack(line, 16), ("x", "yh", "yl"), 0, 0)
    up3, down3 = shift(up2, 1), shift(down2, -1)
    w_all = jnp.zeros((8,) + w_own.shape, w_own.dtype)
    for k, v in ((0, w_own), (1, up1), (7, down1)):
        w_all = lax.dynamic_update_index_in_dim(w_all, v, (zi - k) % 8, 0)
    own, up2, down2, w_all = tie((own, up2, down2, w_all))

    oth = lax.ppermute(own, "c", [(0, 1), (1, 0)])
    starts = jnp.sum(
        documents[None, :] < jnp.arange(DOCS, dtype=jnp.int32)[:, None], axis=1, dtype=jnp.int32
    )
    spans = jnp.arange(span_order.shape[0], dtype=jnp.int32)
    where = (spans // 16 * 2 + spans % 2) * 8 + spans // 2 % 8
    stored = jnp.sum(jnp.where(span_order[None, :] == spans[:, None], where[None, :], 0), axis=1)
    slot = jnp.concatenate(
        [lax.dynamic_slice_in_dim(span_order, 2 * (place * 8 + zi), 2), core[None].astype(jnp.int32)]
    )
    head_out = attention(starts, stored, slot, queries, w_uv, own, oth)
    head_out, up3, down3 = tie((head_out, up3, down3))

    far = jnp.concatenate([shift(up3[:half], 1), shift(down3[half:], -1)], axis=0)
    tokens = head_out.shape[1]
    rows = lax.all_to_all(head_out, row_axes, 0, 0).reshape(COPIES * tokens, head_out.shape[2])
    for k, v in ((2, up2), (6, down2), (3, up3), (5, down3), (4, far)):
        w_all = lax.dynamic_update_index_in_dim(w_all, v, (zi - k) % 8, 0)
    w_cols = w_all.reshape(-1, w_own.shape[1])
    terms = lax.dot_general(
        rows, w_cols, (((1,), (1,)), ((), ())), preferred_element_type=jnp.float32
    ).astype(jnp.bfloat16)
    width = terms.shape[1]
    terms = terms.reshape(2, 4, tokens, width)

    kept = lax.dynamic_index_in_dim(terms, core, 0, keepdims=False)
    sent = lax.dynamic_index_in_dim(terms, 1 - core, 0, keepdims=False)
    got = lax.ppermute(sent, "c", [(0, 1), (1, 0)])
    both = (kept.astype(jnp.float32) + got.astype(jnp.float32)).astype(jnp.bfloat16)

    slot = (place % 2) * 2 + ai("yl")
    left = jnp.zeros((tokens, width), jnp.float32)
    right = left
    for k in range(4):
        pairs = []
        for r in range(8):
            for yl in range(2):
                for c in range(2):
                    i = ((r % 2) * 2 + yl + k) % 4
                    pairs.append((r * 4 + yl * 2 + c, (c * 4 + i) * 4 + r // 2))
        block = lax.dynamic_index_in_dim(both, (slot + k) % 4, 0, keepdims=False)
        got = lax.ppermute(block, ("x", "yh", "yl", "c"), pairs).astype(jnp.float32)
        first_half = (place - k) % 4 < 2
        left = left + jnp.where(first_half, got, 0.0)
        right = right + jnp.where(first_half, 0.0, got)
    return jnp.concatenate([left, right], axis=1).astype(jnp.bfloat16)


def solution(mesh):
    fine = Mesh(mesh.devices.reshape(SIZES), AXES)
    ctx, head = ("x", "yh", "z"), ("yl", "c")
    return jax.shard_map(
        shards,
        mesh=fine,
        in_specs=(
            P(ctx, head, None),
            P(ctx, None),
            P(),
            P(),
            P(head, None, None),
            P(head, ctx),
        ),
        out_specs=P(ctx, head),
        check_vma=False,
    )
```

```python
import functools

import jax
import jax.numpy as jnp
from jax import lax
from jax.experimental import pallas as pl
from jax.experimental.pallas import tpu as pltpu
from jax.sharding import Mesh, PartitionSpec as P

ROPE = 64
VD = 128
DOCS = 6
AXES = ("x", "yh", "z", "yl", "c")
SIZES = (4, 2, 8, 2, 2)
SPAN = 32
HALF = SPAN // 2
GROUP = 16
KEYS = SPAN * GROUP
MAXB = 5
NEG = -1e30
COPIES = 8


def attention_kernel(
    starts, place, slot, q_hbm, w_hbm, own_ref, oth_ref, out_ref,
    k_buf, s_buf, top_buf, sum_buf, acc, mixed, q_ref, w_buf, head_out, q_sem, w_sem, out_sem,
):
    span_total = place.shape[0]
    heads = q_hbm.shape[1]
    q_copy = pltpu.make_async_copy(q_hbm, q_ref, q_sem)
    q_copy.start()
    rows = SPAN * heads
    value_cols = w_hbm.shape[1]
    scale = (VD + ROPE) ** (-0.5) * 1.4426950408889634
    core = slot[2]
    line_rows = 8 * HALF
    low_lanes = lax.broadcasted_iota(jnp.int32, (HALF, 2 * ROPE), 1) < ROPE

    w_copy = pltpu.make_async_copy(w_hbm, w_buf, w_sem)
    w_copy.start()

    def doc_start(pos):
        lo = jnp.zeros_like(pos)
        for d in range(DOCS):
            lo = jnp.maximum(lo, jnp.where(starts[d] <= pos, starts[d], 0))
        return lo

    lane = lax.broadcasted_iota(jnp.int32, (1, KEYS), 1)
    key_half = jnp.where(lane < KEYS // 2, core, 1 - core)
    key_place = ((lane & (KEYS // 2 - 1)) >> 4) * SPAN + key_half * HALF + (lane & (HALF - 1))

    for t in range(2):
        last = slot[t]
        lo = jnp.int32(0)
        for d in range(DOCS):
            lo = jnp.maximum(lo, jnp.where(starts[d] <= last * SPAN, starts[d], 0))
        first = lo // SPAN
        blocks = (last - first + GROUP) // GROUP
        row_token = lax.broadcasted_iota(jnp.int32, (rows, 1), 0) // heads
        q_pos = last * SPAN + row_token
        q_lo = doc_start(q_pos) - first * SPAN
        q_hi = q_pos - first * SPAN
        if t == 0:
            q_copy.wait()
        q = q_ref[t * SPAN : (t + 1) * SPAN].reshape(rows, q_ref.shape[2])
        q = jnp.concatenate([q, q[:, value_cols:]], axis=1)
        top_buf[...] = jnp.full(top_buf.shape, NEG, jnp.float32)
        sum_buf[...] = jnp.zeros(sum_buf.shape, jnp.float32)
        acc[...] = jnp.zeros(acc.shape, jnp.float32)

        def score(b, carry):
            for g in range(GROUP):
                code = place[jnp.minimum(first + b * GROUP + g, span_total - 1)]
                block = lax.shift_right_logical(code, 3)
                z = code & 7
                for i, ref in enumerate((own_ref, oth_ref)):
                    row = i * KEYS // 2 + g * HALF
                    for j in range(value_cols // 128):
                        src = pl.multiple_of(j * line_rows + z * HALF, HALF)
                        k_buf[b, row : row + HALF, j * 128 : (j + 1) * 128] = ref[
                            block, pl.ds(src, HALF)
                        ]
                    src = pl.multiple_of(value_cols // 128 * line_rows + (z & 3) * HALF, HALF)
                    rope = ref[block, pl.ds(src, HALF)]
                    k_buf[b, row : row + HALF, value_cols:] = jnp.where(
                        low_lanes == (z < 4), rope, jnp.zeros_like(rope)
                    )
            s = lax.dot_general(
                q, k_buf[b], (((1,), (1,)), ((), ())), preferred_element_type=jnp.float32
            )
            k_pos = b * KEYS + key_place
            s = jnp.where((k_pos >= q_lo) & (k_pos <= q_hi), s, NEG)
            s_buf[b] = s
            top = top_buf[...]
            for j in range(KEYS // 128):
                top = jnp.maximum(top, s[:, j * 128 : (j + 1) * 128])
            top_buf[...] = top
            return carry

        lax.fori_loop(0, blocks, score, 0)
        top = jnp.max(top_buf[...], axis=1, keepdims=True)

        def mix(b, carry):
            w = jnp.exp2((s_buf[b] - top) * scale)
            part = sum_buf[...]
            for j in range(KEYS // 128):
                part = part + w[:, j * 128 : (j + 1) * 128]
            sum_buf[...] = part
            acc[...] += jnp.dot(
                w.astype(jnp.bfloat16), k_buf[b, :, :value_cols], preferred_element_type=jnp.float32
            )
            return carry

        lax.fori_loop(0, blocks, mix, 0)
        total = jnp.sum(sum_buf[...], axis=1, keepdims=True)
        scaled = acc[...] * (1.0 / total)
        for j in range(value_cols // 128):
            mixed[j, t * rows : (t + 1) * rows, :] = scaled[:, j * 128 : (j + 1) * 128]

    w_copy.wait()
    tokens = 2 * SPAN
    for h in range(0, heads, 2):
        pair = jnp.concatenate(
            [
                jnp.concatenate(
                    [mixed[j, pl.ds(h + i, tokens, stride=heads), :] for j in range(value_cols // 128)],
                    axis=1,
                )
                for i in range(2)
            ],
            axis=0,
        ).astype(jnp.bfloat16)
        both = jnp.dot(
            pair,
            jnp.concatenate([w_buf[h], w_buf[h + 1]], axis=1),
            preferred_element_type=jnp.float32,
        ).astype(jnp.bfloat16)
        head_out[:, h * VD : (h + 1) * VD] = both[:tokens, :VD]
        head_out[:, (h + 1) * VD : (h + 2) * VD] = both[tokens:, VD:]
    copies = [
        pltpu.make_async_copy(head_out, out_ref.at[r], out_sem.at[r])
        for r in range(out_ref.shape[0])
    ]
    for copy in copies:
        copy.start()
    for copy in copies:
        copy.wait()


def in_hbm(v):
    return pltpu.with_memory_space_constraint(v, pltpu.HBM)


def attention(starts, place, slot, queries, w_uv, own, oth):
    tokens, heads, lat = queries.shape
    value_cols = w_uv.shape[1]
    rows = SPAN * heads
    smem = pl.BlockSpec(memory_space=pltpu.SMEM)
    vmem = pl.BlockSpec(memory_space=pltpu.VMEM)
    hbm = pl.BlockSpec(memory_space=pl.ANY)
    return pl.pallas_call(
        attention_kernel,
        out_shape=pltpu.HBM((COPIES, tokens, heads * VD), jnp.bfloat16),
        in_specs=[smem, smem, smem, hbm, hbm, vmem, vmem],
        out_specs=hbm,
        scratch_shapes=[
            pltpu.VMEM((MAXB, KEYS, lat + ROPE), jnp.bfloat16),
            pltpu.VMEM((MAXB, rows, KEYS), jnp.float32),
            pltpu.VMEM((rows, 128), jnp.float32),
            pltpu.VMEM((rows, 128), jnp.float32),
            pltpu.VMEM((rows, value_cols), jnp.float32),
            pltpu.VMEM((value_cols // 128, 2 * rows, 128), jnp.float32),
            pltpu.VMEM(queries.shape, jnp.bfloat16),
            pltpu.VMEM(w_uv.shape, jnp.bfloat16),
            pltpu.VMEM((tokens, heads * VD), jnp.bfloat16),
            pltpu.SemaphoreType.DMA(()),
            pltpu.SemaphoreType.DMA(()),
            pltpu.SemaphoreType.DMA((COPIES,)),
        ],
        compiler_params=pltpu.CompilerParams(vmem_limit_bytes=36 * 2**20),
        cost_estimate=pl.CostEstimate(
            flops=5_000_000_000, bytes_accessed=8_000_000, transcendentals=2_000_000
        ),
    )(starts, place, slot, in_hbm(queries), in_hbm(w_uv), own, oth)


def pack_kernel(line_ref, out_ref, buf, sem):
    blocks, rows, width = line_ref.shape
    count = blocks * rows
    value_cols = width - ROPE
    for j in range(value_cols // 128):
        buf[j * count : (j + 1) * count] = line_ref[:, :, j * 128 : (j + 1) * 128].reshape(count, 128)
    rope = line_ref[:, :, value_cols:].reshape(count, ROPE)
    first = value_cols // 128 * count
    buf[first : first + count // 2] = jnp.concatenate(
        [rope[: count // 2], rope[count // 2 :]], axis=1
    )
    copies = [
        pltpu.make_async_copy(buf, out_ref.at[r], sem.at[r]) for r in range(out_ref.shape[0])
    ]
    for copy in copies:
        copy.start()
    for copy in copies:
        copy.wait()


def pack(line, count):
    rows = line.shape[0] * line.shape[1] * line.shape[2] // 128
    return pl.pallas_call(
        pack_kernel,
        out_shape=pltpu.HBM((count, rows, 128), jnp.bfloat16),
        in_specs=[pl.BlockSpec(memory_space=pltpu.VMEM)],
        out_specs=pl.BlockSpec(memory_space=pl.ANY),
        scratch_shapes=[
            pltpu.VMEM((rows, 128), jnp.bfloat16),
            pltpu.SemaphoreType.DMA((count,)),
        ],
        compiler_params=pltpu.CompilerParams(vmem_limit_bytes=16 * 2**20),
        cost_estimate=pl.CostEstimate(flops=0, bytes_accessed=3_000_000, transcendentals=0),
    )(line)


def gather_rows(v, axes, count):
    return lax.all_to_all(jnp.broadcast_to(v[None], (count,) + v.shape), axes, 0, 0)


def shards(queries, latent, documents, span_order, w_uv, w_out):
    row_axes = ("x", "yh")
    ai = lax.axis_index
    core, zi = ai("c"), ai("z")
    place = ai("x") * 2 + ai("yh")
    tie = lax.optimization_barrier

    def shift(v, k):
        return lax.ppermute(v, "z", [(i, (i + k) % 8) for i in range(8)])

    w_own = w_out.T
    half = 64
    quarter = ai("yl") * 2 + core
    line = gather_rows(lax.dynamic_slice_in_dim(latent, quarter * HALF, HALF), "z", 8)
    line, w_own = tie((line, w_own))

    up1, down1 = shift(w_own, 1), shift(w_own, -1)
    up2, down2 = shift(up1, 1), shift(down1, -1)
    own = lax.all_to_all(pack(line, 16), ("x", "yh", "yl"), 0, 0)
    up3, down3 = shift(up2, 1), shift(down2, -1)
    w_all = jnp.zeros((8,) + w_own.shape, w_own.dtype)
    for k, v in ((0, w_own), (1, up1), (7, down1)):
        w_all = lax.dynamic_update_index_in_dim(w_all, v, (zi - k) % 8, 0)
    own, up2, down2, w_all = tie((own, up2, down2, w_all))

    oth = lax.ppermute(own, "c", [(0, 1), (1, 0)])
    starts = jnp.sum(
        documents[None, :] < jnp.arange(DOCS, dtype=jnp.int32)[:, None], axis=1, dtype=jnp.int32
    )
    spans = jnp.arange(span_order.shape[0], dtype=jnp.int32)
    where = (spans // 16 * 2 + spans % 2) * 8 + spans // 2 % 8
    stored = jnp.sum(jnp.where(span_order[None, :] == spans[:, None], where[None, :], 0), axis=1)
    slot = jnp.concatenate(
        [lax.dynamic_slice_in_dim(span_order, 2 * (place * 8 + zi), 2), core[None].astype(jnp.int32)]
    )
    head_out = attention(starts, stored, slot, queries, w_uv, own, oth)
    head_out, up3, down3 = tie((head_out, up3, down3))

    far = jnp.concatenate([shift(up3[:half], 1), shift(down3[half:], -1)], axis=0)
    tokens = head_out.shape[1]
    rows = lax.all_to_all(head_out, row_axes, 0, 0).reshape(COPIES * tokens, head_out.shape[2])
    for k, v in ((2, up2), (6, down2), (3, up3), (5, down3), (4, far)):
        w_all = lax.dynamic_update_index_in_dim(w_all, v, (zi - k) % 8, 0)
    w_cols = w_all.reshape(-1, w_own.shape[1])
    terms = lax.dot_general(
        rows, w_cols, (((1,), (1,)), ((), ())), preferred_element_type=jnp.float32
    ).astype(jnp.bfloat16)
    width = terms.shape[1]
    terms = terms.reshape(2, 2, 2, tokens, width)

    kept = lax.dynamic_index_in_dim(terms, core, 1, keepdims=False)
    sent = lax.dynamic_index_in_dim(terms, 1 - core, 1, keepdims=False)
    got = lax.ppermute(sent, "c", [(0, 1), (1, 0)])
    both = (kept.astype(jnp.float32) + got.astype(jnp.float32)).astype(jnp.bfloat16)
    both = both.reshape(4, tokens, width)

    slot = ai("yl") * 2 + ai("yh")
    left = jnp.zeros((tokens, width), jnp.float32)
    right = left
    for k in range(4):
        pairs = []
        for r in range(8):
            for yl in range(2):
                for c in range(2):
                    i = (yl * 2 + r % 2) ^ k
                    pairs.append((r * 4 + yl * 2 + c, (i // 2 * 4 + c * 2 + i % 2) * 4 + r // 2))
        block = lax.dynamic_index_in_dim(both, slot ^ k, 0, keepdims=False)
        got = lax.ppermute(block, ("x", "yh", "yl", "c"), pairs).astype(jnp.float32)
        first_half = (ai("yh") ^ (k & 1)) == 0
        left = left + jnp.where(first_half, got, 0.0)
        right = right + jnp.where(first_half, 0.0, got)
    return jnp.concatenate([left, right], axis=1).astype(jnp.bfloat16)


def solution(mesh):
    fine = Mesh(mesh.devices.reshape(SIZES), AXES)
    ctx, head = ("x", "yh", "z"), ("yl", "c")
    return jax.shard_map(
        shards,
        mesh=fine,
        in_specs=(
            P(ctx, head, None),
            P(ctx, None),
            P(),
            P(),
            P(head, None, None),
            P(head, ctx),
        ),
        out_specs=P(ctx, head),
        check_vma=False,
    )
```

```python
import functools

import jax
import jax.numpy as jnp
from jax import lax
from jax.experimental import pallas as pl
from jax.experimental.pallas import tpu as pltpu
from jax.sharding import Mesh, PartitionSpec as P

ROPE = 64
VD = 128
DOCS = 6
AXES = ("x", "yh", "z", "yl", "c")
SIZES = (4, 2, 8, 2, 2)
SPAN = 32
HALF = SPAN // 2
GROUP = 16
KEYS = SPAN * GROUP
MAXB = 5
NEG = -1e30
COPIES = 8


def attention_kernel(
    starts, place, slot, q_hbm, w_hbm, own_ref, oth_ref, out_ref,
    k_buf, s_buf, top_buf, sum_buf, acc, mixed, q_ref, w_buf, head_out, q_sem, w_sem, out_sem,
):
    span_total = place.shape[0]
    heads = q_hbm.shape[1]
    q_copy = pltpu.make_async_copy(q_hbm, q_ref, q_sem)
    q_copy.start()
    rows = SPAN * heads
    value_cols = w_hbm.shape[1]
    scale = (VD + ROPE) ** (-0.5) * 1.4426950408889634
    core = slot[2]
    line_rows = 8 * HALF
    low_lanes = lax.broadcasted_iota(jnp.int32, (HALF, 2 * ROPE), 1) < ROPE

    w_copy = pltpu.make_async_copy(w_hbm, w_buf, w_sem)
    w_copy.start()

    def doc_start(pos):
        lo = jnp.zeros_like(pos)
        for d in range(DOCS):
            lo = jnp.maximum(lo, jnp.where(starts[d] <= pos, starts[d], 0))
        return lo

    def key_places(keys):
        lane = lax.broadcasted_iota(jnp.int32, (1, keys), 1)
        key_half = jnp.where(lane < keys // 2, core, 1 - core)
        return ((lane & (keys // 2 - 1)) >> 4) * SPAN + key_half * HALF + (lane & (HALF - 1))

    for t in range(2):
        last = slot[t]
        lo = jnp.int32(0)
        for d in range(DOCS):
            lo = jnp.maximum(lo, jnp.where(starts[d] <= last * SPAN, starts[d], 0))
        first = lo // SPAN
        spans = last - first + 1
        left = spans & (GROUP - 1)
        blocks = (spans + GROUP // 2 - 1) // GROUP
        tail = (left > 0) & (left <= GROUP // 2)
        row_token = lax.broadcasted_iota(jnp.int32, (rows, 1), 0) // heads
        q_pos = last * SPAN + row_token
        q_lo = doc_start(q_pos) - first * SPAN
        q_hi = q_pos - first * SPAN
        if t == 0:
            q_copy.wait()
        q = q_ref[t * SPAN : (t + 1) * SPAN].reshape(rows, q_ref.shape[2])
        q = jnp.concatenate([q, q[:, value_cols:]], axis=1)
        top_buf[...] = jnp.full(top_buf.shape, NEG, jnp.float32)
        sum_buf[...] = jnp.zeros(sum_buf.shape, jnp.float32)
        acc[...] = jnp.zeros(acc.shape, jnp.float32)

        def score(b, group):
            keys = group * SPAN
            for g in range(group):
                code = place[jnp.minimum(first + b * GROUP + g, span_total - 1)]
                block = lax.shift_right_logical(code, 3)
                z = code & 7
                for i, ref in enumerate((own_ref, oth_ref)):
                    row = i * keys // 2 + g * HALF
                    for j in range(value_cols // 128):
                        src = pl.multiple_of(j * line_rows + z * HALF, HALF)
                        k_buf[b, row : row + HALF, j * 128 : (j + 1) * 128] = ref[
                            block, pl.ds(src, HALF)
                        ]
                    src = pl.multiple_of(value_cols // 128 * line_rows + (z & 3) * HALF, HALF)
                    rope = ref[block, pl.ds(src, HALF)]
                    k_buf[b, row : row + HALF, value_cols:] = jnp.where(
                        low_lanes == (z < 4), rope, jnp.zeros_like(rope)
                    )
            s = lax.dot_general(
                q, k_buf[b, :keys], (((1,), (1,)), ((), ())), preferred_element_type=jnp.float32
            )
            k_pos = b * KEYS + key_places(keys)
            s = jnp.where((k_pos >= q_lo) & (k_pos <= q_hi), s, NEG)
            s_buf[b, :, :keys] = s
            top = top_buf[...]
            for j in range(keys // 128):
                top = jnp.maximum(top, s[:, j * 128 : (j + 1) * 128])
            top_buf[...] = top

        def each(step):
            def whole(b, carry):
                step(b, GROUP)
                return carry

            lax.fori_loop(0, blocks, whole, 0)

            @pl.when(tail)
            def _():
                step(blocks, GROUP // 2)

        each(score)
        top = jnp.max(top_buf[...], axis=1, keepdims=True)

        def mix(b, group):
            keys = group * SPAN
            w = jnp.exp2((s_buf[b, :, :keys] - top) * scale)
            part = sum_buf[...]
            for j in range(keys // 128):
                part = part + w[:, j * 128 : (j + 1) * 128]
            sum_buf[...] = part
            acc[...] += jnp.dot(
                w.astype(jnp.bfloat16), k_buf[b, :keys, :value_cols], preferred_element_type=jnp.float32
            )

        each(mix)
        total = jnp.sum(sum_buf[...], axis=1, keepdims=True)
        scaled = acc[...] * (1.0 / total)
        for j in range(value_cols // 128):
            mixed[j, t * rows : (t + 1) * rows, :] = scaled[:, j * 128 : (j + 1) * 128]

    w_copy.wait()
    tokens = 2 * SPAN
    for h in range(0, heads, 2):
        pair = jnp.concatenate(
            [
                jnp.concatenate(
                    [mixed[j, pl.ds(h + i, tokens, stride=heads), :] for j in range(value_cols // 128)],
                    axis=1,
                )
                for i in range(2)
            ],
            axis=0,
        ).astype(jnp.bfloat16)
        both = jnp.dot(
            pair,
            jnp.concatenate([w_buf[h], w_buf[h + 1]], axis=1),
            preferred_element_type=jnp.float32,
        ).astype(jnp.bfloat16)
        head_out[:, h * VD : (h + 1) * VD] = both[:tokens, :VD]
        head_out[:, (h + 1) * VD : (h + 2) * VD] = both[tokens:, VD:]
    copies = [
        pltpu.make_async_copy(head_out, out_ref.at[r], out_sem.at[r])
        for r in range(out_ref.shape[0])
    ]
    for copy in copies:
        copy.start()
    for copy in copies:
        copy.wait()


def in_hbm(v):
    return pltpu.with_memory_space_constraint(v, pltpu.HBM)


def attention(starts, place, slot, queries, w_uv, own, oth):
    tokens, heads, lat = queries.shape
    value_cols = w_uv.shape[1]
    rows = SPAN * heads
    smem = pl.BlockSpec(memory_space=pltpu.SMEM)
    vmem = pl.BlockSpec(memory_space=pltpu.VMEM)
    hbm = pl.BlockSpec(memory_space=pl.ANY)
    return pl.pallas_call(
        attention_kernel,
        out_shape=pltpu.HBM((COPIES, tokens, heads * VD), jnp.bfloat16),
        in_specs=[smem, smem, smem, hbm, hbm, vmem, vmem],
        out_specs=hbm,
        scratch_shapes=[
            pltpu.VMEM((MAXB, KEYS, lat + ROPE), jnp.bfloat16),
            pltpu.VMEM((MAXB, rows, KEYS), jnp.float32),
            pltpu.VMEM((rows, 128), jnp.float32),
            pltpu.VMEM((rows, 128), jnp.float32),
            pltpu.VMEM((rows, value_cols), jnp.float32),
            pltpu.VMEM((value_cols // 128, 2 * rows, 128), jnp.float32),
            pltpu.VMEM(queries.shape, jnp.bfloat16),
            pltpu.VMEM(w_uv.shape, jnp.bfloat16),
            pltpu.VMEM((tokens, heads * VD), jnp.bfloat16),
            pltpu.SemaphoreType.DMA(()),
            pltpu.SemaphoreType.DMA(()),
            pltpu.SemaphoreType.DMA((COPIES,)),
        ],
        compiler_params=pltpu.CompilerParams(vmem_limit_bytes=36 * 2**20),
        cost_estimate=pl.CostEstimate(
            flops=5_000_000_000, bytes_accessed=8_000_000, transcendentals=2_000_000
        ),
    )(starts, place, slot, in_hbm(queries), in_hbm(w_uv), own, oth)


def pack_kernel(line_ref, out_ref, buf, sem):
    blocks, rows, width = line_ref.shape
    count = blocks * rows
    value_cols = width - ROPE
    for j in range(value_cols // 128):
        buf[j * count : (j + 1) * count] = line_ref[:, :, j * 128 : (j + 1) * 128].reshape(count, 128)
    rope = line_ref[:, :, value_cols:].reshape(count, ROPE)
    first = value_cols // 128 * count
    buf[first : first + count // 2] = jnp.concatenate(
        [rope[: count // 2], rope[count // 2 :]], axis=1
    )
    copies = [
        pltpu.make_async_copy(buf, out_ref.at[r], sem.at[r]) for r in range(out_ref.shape[0])
    ]
    for copy in copies:
        copy.start()
    for copy in copies:
        copy.wait()


def pack(line, count):
    rows = line.shape[0] * line.shape[1] * line.shape[2] // 128
    return pl.pallas_call(
        pack_kernel,
        out_shape=pltpu.HBM((count, rows, 128), jnp.bfloat16),
        in_specs=[pl.BlockSpec(memory_space=pltpu.VMEM)],
        out_specs=pl.BlockSpec(memory_space=pl.ANY),
        scratch_shapes=[
            pltpu.VMEM((rows, 128), jnp.bfloat16),
            pltpu.SemaphoreType.DMA((count,)),
        ],
        compiler_params=pltpu.CompilerParams(vmem_limit_bytes=16 * 2**20),
        cost_estimate=pl.CostEstimate(flops=0, bytes_accessed=3_000_000, transcendentals=0),
    )(line)


def gather_rows(v, axes, count):
    return lax.all_to_all(jnp.broadcast_to(v[None], (count,) + v.shape), axes, 0, 0)


def shards(queries, latent, documents, span_order, w_uv, w_out):
    row_axes = ("x", "yh")
    ai = lax.axis_index
    core, zi = ai("c"), ai("z")
    place = ai("x") * 2 + ai("yh")
    tie = lax.optimization_barrier

    def shift(v, k):
        return lax.ppermute(v, "z", [(i, (i + k) % 8) for i in range(8)])

    w_own = w_out.T
    half = 64
    quarter = ai("yl") * 2 + core
    line = gather_rows(lax.dynamic_slice_in_dim(latent, quarter * HALF, HALF), "z", 8)
    line, w_own = tie((line, w_own))

    up1, down1 = shift(w_own, 1), shift(w_own, -1)
    up2, down2 = shift(up1, 1), shift(down1, -1)
    own = lax.all_to_all(pack(line, 16), ("x", "yh", "yl"), 0, 0)
    up3, down3 = shift(up2, 1), shift(down2, -1)
    w_all = jnp.zeros((8,) + w_own.shape, w_own.dtype)
    for k, v in ((0, w_own), (1, up1), (7, down1)):
        w_all = lax.dynamic_update_index_in_dim(w_all, v, (zi - k) % 8, 0)
    own, up2, down2, w_all = tie((own, up2, down2, w_all))

    oth = lax.ppermute(own, "c", [(0, 1), (1, 0)])
    starts = jnp.sum(
        documents[None, :] < jnp.arange(DOCS, dtype=jnp.int32)[:, None], axis=1, dtype=jnp.int32
    )
    spans = jnp.arange(span_order.shape[0], dtype=jnp.int32)
    where = (spans // 16 * 2 + spans % 2) * 8 + spans // 2 % 8
    stored = jnp.sum(jnp.where(span_order[None, :] == spans[:, None], where[None, :], 0), axis=1)
    slot = jnp.concatenate(
        [lax.dynamic_slice_in_dim(span_order, 2 * (place * 8 + zi), 2), core[None].astype(jnp.int32)]
    )
    head_out = attention(starts, stored, slot, queries, w_uv, own, oth)
    head_out, up3, down3 = tie((head_out, up3, down3))

    far = jnp.concatenate([shift(up3[:half], 1), shift(down3[half:], -1)], axis=0)
    tokens = head_out.shape[1]
    rows = lax.all_to_all(head_out, row_axes, 0, 0).reshape(COPIES * tokens, head_out.shape[2])
    for k, v in ((2, up2), (6, down2), (3, up3), (5, down3), (4, far)):
        w_all = lax.dynamic_update_index_in_dim(w_all, v, (zi - k) % 8, 0)
    w_cols = w_all.reshape(-1, w_own.shape[1])
    terms = lax.dot_general(
        rows, w_cols, (((1,), (1,)), ((), ())), preferred_element_type=jnp.float32
    ).astype(jnp.bfloat16)
    width = terms.shape[1]
    terms = terms.reshape(2, 2, 2, tokens, width)

    kept = lax.dynamic_index_in_dim(terms, core, 1, keepdims=False)
    sent = lax.dynamic_index_in_dim(terms, 1 - core, 1, keepdims=False)
    got = lax.ppermute(sent, "c", [(0, 1), (1, 0)])
    both = (kept.astype(jnp.float32) + got.astype(jnp.float32)).astype(jnp.bfloat16)
    both = both.reshape(4, tokens, width)

    slot = ai("yl") * 2 + ai("yh")
    left = jnp.zeros((tokens, width), jnp.float32)
    right = left
    for k in range(4):
        pairs = []
        for r in range(8):
            for yl in range(2):
                for c in range(2):
                    i = (yl * 2 + r % 2) ^ k
                    pairs.append((r * 4 + yl * 2 + c, (i // 2 * 4 + c * 2 + i % 2) * 4 + r // 2))
        block = lax.dynamic_index_in_dim(both, slot ^ k, 0, keepdims=False)
        got = lax.ppermute(block, ("x", "yh", "yl", "c"), pairs).astype(jnp.float32)
        first_half = (ai("yh") ^ (k & 1)) == 0
        left = left + jnp.where(first_half, got, 0.0)
        right = right + jnp.where(first_half, 0.0, got)
    return jnp.concatenate([left, right], axis=1).astype(jnp.bfloat16)


def solution(mesh):
    fine = Mesh(mesh.devices.reshape(SIZES), AXES)
    ctx, head = ("x", "yh", "z"), ("yl", "c")
    return jax.shard_map(
        shards,
        mesh=fine,
        in_specs=(
            P(ctx, head, None),
            P(ctx, None),
            P(),
            P(),
            P(head, None, None),
            P(head, ctx),
        ),
        out_specs=P(ctx, head),
        check_vma=False,
    )
```
